128 devices in a mesh: dp: 32 (over x, y, z_hi), tensor: 4 (over z_lo, core).
Axes of the slice: x: 4, y: 4, z: 4 (z_hi: 2, z_lo: 2; z = z_hi * 2 + z_lo), core: 2. Of those that a mesh axis runs over, the one named last changes fastest.
Arguments:
- input_frames: bfloat16 [32768, 768], P(('dp', 'tensor')), may hold values from -6 to 6
- cotangent: bfloat16 [32768, 768], P(('dp', 'tensor')), may hold values from -24 to 24
- attention_in: bfloat16 [2, 3, 768, 768], P(None, None, 'dp', 'tensor'), may hold values from -0.21875 to 0.21875
- attention_bias: bfloat16 [2, 2, 768], P(None, None, ('tensor', 'dp')), may hold values from -3 to 3
- attention_out: bfloat16 [2, 768, 768], P(None, 'tensor', 'dp'), may hold values from -0.4375 to 0.4375
- up_weight: bfloat16 [2, 768, 3072], P(None, 'dp', 'tensor'), may hold values from -0.21875 to 0.21875
- up_bias: bfloat16 [2, 3072], P(None, ('tensor', 'dp')), may hold values from -3 to 3
- down_weight: bfloat16 [2, 3072, 768], P(None, 'tensor', 'dp'), may hold values from -0.109375 to 0.109375
- norm_gains: float32 [2, 2, 768], P(None, None, ('dp', 'tensor')), may hold values from 0.1 to 1.9
- row_shifts: float32 [2, 4, 768], P(None, None, ('dp', 'tensor')), may hold values from -2 to 2
Outputs:
- output_frames: float32 [32768, 768], P(('dp', 'tensor'))
- grad_frames: float32 [32768, 768], P(('dp', 'tensor'))
- grad_attention_in: float32 [2, 3, 768, 768], P(None, None, 'dp', 'tensor')
- grad_attention_bias: float32 [2, 2, 768], P(None, None, ('tensor', 'dp'))
- grad_attention_out: float32 [2, 768, 768], P(None, 'tensor', 'dp')
- grad_up_weight: float32 [2, 768, 3072], P(None, 'dp', 'tensor')
- grad_up_bias: float32 [2, 3072], P(None, ('tensor', 'dp'))
- grad_down_weight: float32 [2, 3072, 768], P(None, 'tensor', 'dp')
- grad_norm_gains: float32 [2, 2, 768], P(None, None, ('dp', 'tensor'))
- grad_row_shifts: float32 [2, 4, 768], P(None, None, ('dp', 'tensor'))
The draws below stay inside these ranges and needn't reach their ends.
All inputs are finite; a program needn't handle non-finite values.
Results may differ from the reference program's by a relative error of at most 0.01.
Values may be sent and summed in bfloat16 or wider, within the bound.
No kernel may reach another device: no remote copies, remote signals or barrier semaphores. Data moves between devices by JAX's collectives and lax.ppermute only.
A program may use at most 192 MiB of HBM per device.

```python
import jax
import jax.numpy as jnp
from jax import lax

D = 768
HEADS = 12
HEAD_DIM = 64
FF = 3072
FRAMES = 1024
LAYERS = 2
TOKENS = 32768


def spiked(drawn, key, source, target, parts, factor):
    def block_of(position):
        return (jnp.arange(drawn.shape[position]) // (drawn.shape[position] // parts)).reshape((-1,) + (1,) * (drawn.ndim - 1 - position))

    near = jax.random.permutation(key, parts)[block_of(target)]
    other_side = (block_of(target) + parts // 2) % parts
    return jnp.where((block_of(source) == near) | (block_of(source) == other_side), factor * drawn, drawn)


def level_of(own_key, extent, shards, low, high):
    def one(position, blocks):
        heights = jax.random.uniform(jax.random.fold_in(jax.random.fold_in(own_key, 6), position), (blocks,), jnp.float32, low / len(shards), high / len(shards))
        return jnp.repeat(jnp.exp(heights), extent[position] // blocks).reshape((-1,) + (1,) * (len(extent) - position - 1))

    gain = one(*shards[0])
    for cut in shards[1:]:
        gain = gain * one(*cut)
    return gain


def scatter_about(rng, shape, deviation, bound, split=(), held_as=jnp.bfloat16):
    level = level_of(rng, shape, split, -0.22, 0.18) if split else 1.0
    entries = jax.random.normal(rng, shape, jnp.float32) * deviation * level
    return jnp.minimum(jnp.maximum(entries, -bound), bound).astype(held_as)


def gaussian_with(own_key, extent, scale, most, cuts, heavy, kind=jnp.bfloat16):
    drawn = scale * jax.random.normal(own_key, extent, jnp.float32)
    if cuts:
        drawn = drawn * level_of(own_key, extent, cuts, -0.22, 0.18)
    return jnp.clip(spiked(drawn, jax.random.fold_in(own_key, 3), *heavy), -most, most).astype(kind)


def setup_inputs(seed: int = 0) -> dict:
    keys = jax.random.split(jax.random.key(seed), 11)
    input_frames = scatter_about(keys[0], (TOKENS, D), 1.0, 6.0, ((0, 128),))
    cotangent = gaussian_with(keys[1], (TOKENS, D), 1.0, 24.0, ((0, 128),), (0, 1, 128, 5.5))
    attention_in = scatter_about(keys[2], (LAYERS, 3, D, D), D ** -0.5, 0.21875, ((2, 32), (3, 4)))
    attention_bias = scatter_about(keys[3], (LAYERS, 2, D), 0.5, 3.0, ((2, 128),))
    attention_out = scatter_about(keys[4], (LAYERS, D, D), (D // 4) ** -0.5, 0.4375, ((1, 4), (2, 32)))
    up_weight = scatter_about(keys[5], (LAYERS, D, FF), D ** -0.5, 0.21875, ((1, 32), (2, 4)))
    up_bias = scatter_about(keys[6], (LAYERS, FF), 0.5, 3.0, ((1, 128),))
    down_weight = scatter_about(keys[7], (LAYERS, FF, D), FF ** -0.5, 0.109375, ((1, 4), (2, 32)))
    norm_gains = jnp.clip(1.0 + 0.18 * jax.random.normal(keys[8], (LAYERS, 2, D), jnp.float32), 0.1, 1.9)
    row_shifts = scatter_about(keys[9], (LAYERS, 4, D), 0.3, 2.0, ((2, 128),), jnp.float32)
    return {"input_frames": input_frames, "cotangent": cotangent, "attention_in": attention_in, "attention_bias": attention_bias, "attention_out": attention_out, "up_weight": up_weight, "up_bias": up_bias, "down_weight": down_weight, "norm_gains": norm_gains, "row_shifts": row_shifts}


@jax.custom_vjp
def low(v):
    return lax.optimization_barrier(v.astype(jnp.bfloat16)).astype(jnp.float32)

@jax.custom_vjp
def low_back(v):
    return v

def low_keep(v):
    return (low(v), None)

def low_pass(kept, grad):
    return (grad,)

def back_keep(v):
    return (v, None)

def back_low(kept, grad):
    return (low(grad),)
low.defvjp(low_keep, low_pass)
low_back.defvjp(back_keep, back_low)
norm_eps = 1e-05
highest = lax.Precision.HIGHEST

def product(left_side, right_side):
    return jnp.dot(left_side, right_side, precision=highest, preferred_element_type=jnp.float32)

def layer_norm(stream, gain_row, shift_row):
    row_mean = lax.optimization_barrier(jnp.mean(stream, axis=-1, keepdims=True))
    centred = stream - row_mean
    variance = lax.optimization_barrier(jnp.mean(centred * centred, axis=-1, keepdims=True))
    return centred * lax.rsqrt(variance + norm_eps) * gain_row + shift_row

def encoder_clip(stream, weights):
    attention_in, attention_bias, attention_out, up_weight, up_bias, down_weight, norm_gains, row_shifts = weights
    for layer_index in range(LAYERS):
        normed = low(layer_norm(stream, norm_gains[layer_index, 0], row_shifts[layer_index, 0]))
        queries = low(low_back(product(normed, attention_in[layer_index, 0]) + attention_bias[layer_index, 0]))
        key_rows = low(low_back(product(normed, attention_in[layer_index, 1])))
        values = low(low_back(product(normed, attention_in[layer_index, 2]) + attention_bias[layer_index, 1]))
        queries = queries.reshape(FRAMES, HEADS, HEAD_DIM)
        key_rows = key_rows.reshape(FRAMES, HEADS, HEAD_DIM)
        values = values.reshape(FRAMES, HEADS, HEAD_DIM)
        scores = low_back(jnp.einsum('qhd,khd->hqk', queries, key_rows, precision=highest) * 0.125)
        attention = low(jax.nn.softmax(scores, axis=-1))
        mixture = jnp.einsum('hqk,khd->qhd', attention, values, precision=highest).reshape(FRAMES, D)
        mixture = low(low_back(mixture))
        stream = stream + low_back(product(mixture, attention_out[layer_index])) + row_shifts[layer_index, 1]
        lifted = low(layer_norm(stream, norm_gains[layer_index, 1], row_shifts[layer_index, 2]))
        hidden = low_back(product(lifted, up_weight[layer_index]) + up_bias[layer_index])
        active = low(jax.nn.gelu(hidden, approximate=False))
        stream = stream + low_back(product(active, down_weight[layer_index])) + row_shifts[layer_index, 3]
    return stream

def reference(input_frames, cotangent, attention_in, attention_bias, attention_out, up_weight, up_bias, down_weight, norm_gains, row_shifts):
    weights = (attention_in.astype(jnp.float32), attention_bias.astype(jnp.float32), attention_out.astype(jnp.float32), up_weight.astype(jnp.float32), up_bias.astype(jnp.float32), down_weight.astype(jnp.float32), norm_gains.astype(jnp.float32), row_shifts.astype(jnp.float32))

    def forward(inputs, layer_weights):
        clip_rows = inputs.reshape(-1, FRAMES, D)
        clip_step = jax.checkpoint(lambda clip_data: encoder_clip(clip_data, layer_weights))
        return lax.map(clip_step, clip_rows).reshape(-1, D)
    output, pullback = jax.vjp(forward, input_frames.astype(jnp.float32), weights)
    grad_frames, grad_weights = pullback(cotangent.astype(jnp.float32))
    return (output, grad_frames, grad_weights[0], grad_weights[1], grad_weights[2], grad_weights[3], grad_weights[4], grad_weights[5], grad_weights[6], grad_weights[7])
```

```python
import jax
import jax.numpy as jnp
from jax import lax
from jax.sharding import Mesh, PartitionSpec as P

HEAD_DIM = 64
D = 768
bf16 = jnp.bfloat16
f32 = jnp.float32

norm_eps = 1e-05
score_scale = 0.125
root_half = 0.7071067811865476
inv_root_two_pi = 0.3989422804014327

CHIPS = ("x", "y", "zh", "zl")
ALL = CHIPS + ("core",)
RING = {"x": "x", "y": "y", "z": ("zh", "zl")}


def norm_forward(stream, gain_row, shift_row):
    row_mean = jnp.mean(stream, axis=-1, keepdims=True)
    centred = stream - row_mean
    variance = jnp.mean(centred * centred, axis=-1, keepdims=True)
    inverse = lax.rsqrt(variance + norm_eps)
    scaled = centred * inverse
    return (scaled * gain_row + shift_row, scaled, inverse)


def norm_backward(grad_output, scaled, inverse, gain_row):
    grad_scaled = grad_output * gain_row
    mean_grad = jnp.mean(grad_scaled, axis=-1, keepdims=True)
    mean_cross = jnp.mean(grad_scaled * scaled, axis=-1, keepdims=True)
    grad_input = inverse * (grad_scaled - mean_grad - scaled * mean_cross)
    return (grad_input, jnp.sum(grad_output * scaled, axis=0), jnp.sum(grad_output, axis=0))


def gelu_slope(hidden):
    normal_cdf = 0.5 * (1.0 + lax.erf(hidden * root_half))
    return normal_cdf + hidden * jnp.exp(-0.5 * hidden * hidden) * inv_root_two_pi


def dot(left, right, left_dim, right_dim):
    return lax.dot_general(
        left, right, (((left_dim,), (right_dim,)), ((), ())), preferred_element_type=f32
    )


def split_low(value):
    high = lax.reduce_precision(value, 8, 7)
    return high.astype(bf16), (value - high).astype(bf16)


def core_gather(value):
    return lax.all_gather(value, "core", axis=0, tiled=True)


def core_scatter(partial):
    rows = partial.shape[0] // 2
    core = lax.axis_index("core")
    away = lax.dynamic_slice_in_dim(partial, (1 - core) * rows, rows, 0).astype(bf16)
    kept = lax.dynamic_slice_in_dim(partial, core * rows, rows, 0)
    return kept + lax.ppermute(away, "core", [(0, 1), (1, 0)]).astype(f32)


def swap_zl(value):
    return lax.ppermute(value, "zl", [(0, 1), (1, 0)])


def halve(value, axis):
    me = lax.axis_index(RING[axis])
    pick = lambda index: lax.dynamic_index_in_dim(value, index, 0, False)
    near = [(i, i ^ 1) for i in range(4)]
    far = [(i, i ^ 3) for i in range(4)]
    if axis == "z":
        near, far, one, three = far, near, 3, 1
    else:
        one, three = 1, 3
    sent = jnp.stack([pick(me ^ one), pick(me ^ 2)])
    came = lax.ppermute(sent, RING[axis], near)
    onward = (pick(me ^ three).astype(f32) + came[1].astype(f32)).astype(bf16)
    last = lax.ppermute(onward, RING[axis], far)
    return pick(me).astype(f32) + came[0].astype(f32) + last.astype(f32)


def reduce_stream(value, order):
    dims = ["x", "y", "z"]
    for step, axis in enumerate(order):
        value = halve(jnp.moveaxis(value, dims.index(axis), 0), axis)
        dims.remove(axis)
        if step < 2:
            value = value.astype(bf16)
    return value


def place_stream(halves):
    rows = D // 32
    parts = [half.reshape(4, 4, 2, 1, rows, half.shape[1]) for half in halves]
    return jnp.concatenate(parts, axis=3).reshape(4, 4, 4, rows, halves[0].shape[1])


def attend(queries, key_rows, values):
    scores = jnp.einsum("qhd,khd->hqk", queries, key_rows, preferred_element_type=f32)
    scores = scores * score_scale
    row_max = jnp.max(scores, axis=-1, keepdims=True)
    shifted = jnp.exp(scores - row_max)
    total = jnp.sum(shifted, axis=-1, keepdims=True)
    attention = (shifted / total).astype(bf16)
    mixture = jnp.einsum("hqk,khd->qhd", attention, values, preferred_element_type=f32)
    return mixture.astype(bf16), row_max + jnp.log(total)


def attend_back(queries, key_rows, values, log_sum, grad_mixture):
    scores = jnp.einsum("qhd,khd->hqk", queries, key_rows, preferred_element_type=f32)
    attention = jnp.exp(scores * score_scale - log_sum)
    grad_attention = jnp.einsum("qhd,khd->hqk", grad_mixture, values, preferred_element_type=f32)
    row_delta = jnp.sum(attention * grad_attention, axis=-1, keepdims=True)
    grad_scores = (attention * (grad_attention - row_delta)).astype(bf16)
    grad_queries = jnp.einsum("hqk,khd->qhd", grad_scores, key_rows, preferred_element_type=f32)
    grad_keys = jnp.einsum("hqk,qhd->khd", grad_scores, queries, preferred_element_type=f32)
    grad_values = jnp.einsum(
        "hqk,qhd->khd", attention.astype(bf16), grad_mixture, preferred_element_type=f32
    )
    return grad_queries * score_scale, grad_keys * score_scale, grad_values


def per_device(
    input_frames,
    cotangent,
    attention_in,
    attention_bias,
    attention_out,
    up_weight,
    up_bias,
    down_weight,
    norm_gains,
    row_shifts,
):
    layers = attention_in.shape[0]
    core = lax.axis_index("core")
    rows = D // 32

    gains_shifts = jnp.concatenate([norm_gains.reshape(4, 6), row_shifts.reshape(8, 6)], axis=0)
    both_cores = lax.all_gather(gains_shifts, "core", axis=0)
    high, low = split_low(both_cores)
    small = jnp.concatenate([high[0], low[0], high[1], low[1]], axis=1)
    biases = jnp.concatenate([attention_bias.reshape(4, 6), up_bias.reshape(8, 6)], axis=0)
    small = jnp.concatenate([small, jnp.pad(biases, ((0, 0), (0, 18)))], axis=0)
    small = jnp.pad(small, ((0, 0), (0, 104)))

    def packed(layer):
        return jnp.concatenate(
            [
                down_weight[layer].T,
                up_weight[layer],
                attention_in[layer, 0],
                attention_in[layer, 1],
                attention_in[layer, 2],
                attention_out[layer].T,
            ],
            axis=1,
        )

    gathered = []
    for layer in range(layers):
        block = packed(layer)
        if layer == 0:
            block = jnp.concatenate([block, small], axis=1)
        whole = lax.all_gather(block, CHIPS, axis=0, tiled=True)
        gathered.append(whole.reshape(32, 2, rows, block.shape[1]))

    def columns(layer, first, last):
        halves = [gathered[layer][:, z, :, first:last].reshape(D, last - first) for z in range(2)]
        return jnp.concatenate(halves, axis=1)

    tiny = gathered[0][:, :, :, 2304:2328].astype(f32)
    by_core = tiny[:, :, :12].reshape(32, 2, 12, 2, 2, 6)
    full = (by_core[:, :, :, :, 0] + by_core[:, :, :, :, 1]).transpose(2, 0, 1, 3, 4).reshape(12, D)
    full_gains = full[:4].reshape(2, 2, D)
    full_shifts = full[4:].reshape(2, 4, D)
    in_bias = tiny[:, :, 12:16, :6].transpose(2, 1, 0, 3).reshape(2, 2, 2, 192)
    hidden_bias = tiny[:, :, 16:24, :6].reshape(32, 2, 2, 24).transpose(2, 1, 0, 3).reshape(2, 1536)

    def heads(qkv_part):
        return qkv_part.reshape(qkv_part.shape[0], 6, HEAD_DIM)

    stream = input_frames.astype(f32)
    stored = []
    for layer in range(layers):
        w_down = columns(layer, 0, 768)
        w_up = columns(layer, 768, 1536)
        w_qkv = columns(layer, 1536, 2112)
        w_out = columns(layer, 2112, 2304)
        zeros = jnp.zeros((192,), f32)
        qkv_bias = jnp.concatenate(
            [
                in_bias[layer, 0, 0],
                zeros,
                in_bias[layer, 1, 0],
                in_bias[layer, 0, 1],
                zeros,
                in_bias[layer, 1, 1],
            ]
        )
        normed, scaled_one, inverse_one = norm_forward(
            stream, full_gains[layer, 0], full_shifts[layer, 0]
        )
        normed_all = core_gather(normed.astype(bf16))
        qkv = (dot(normed_all, w_qkv, 1, 0) + qkv_bias).astype(bf16)
        queries = jnp.concatenate([qkv[:, 0:192], qkv[:, 576:768]], axis=1)
        pair = jnp.concatenate(
            [qkv[:, 192:384], qkv[:, 768:960], qkv[:, 384:576], qkv[:, 960:1152]], axis=1
        )
        pair_all = jnp.concatenate([pair, swap_zl(pair)], axis=0)
        key_rows, values = pair_all[:, :384], pair_all[:, 384:]
        mixture, log_sum = attend(heads(queries), heads(key_rows), heads(values))
        mixture = mixture.reshape(-1, 384)
        middle = stream + core_scatter(dot(mixture, w_out, 1, 1)) + full_shifts[layer, 1]
        lifted, scaled_two, inverse_two = norm_forward(
            middle, full_gains[layer, 1], full_shifts[layer, 2]
        )
        lifted_all = core_gather(lifted.astype(bf16))
        hidden = dot(lifted_all, w_up, 1, 0) + hidden_bias[layer]
        active = jax.nn.gelu(hidden, approximate=False).astype(bf16)
        stream = middle + core_scatter(dot(active, w_down, 1, 1)) + full_shifts[layer, 3]
        stored.append(
            (
                (w_down, w_up, w_qkv, w_out),
                normed_all,
                scaled_one,
                inverse_one,
                queries,
                key_rows,
                values,
                log_sum,
                mixture,
                scaled_two,
                inverse_two,
                lifted_all,
                hidden,
                active,
            )
        )

    grad_stream = cotangent.astype(f32)
    reduced = [None] * layers
    for layer in reversed(range(layers)):
        (
            (w_down, w_up, w_qkv, w_out),
            normed_all,
            scaled_one,
            inverse_one,
            queries,
            key_rows,
            values,
            log_sum,
            mixture,
            scaled_two,
            inverse_two,
            lifted_all,
            hidden,
            active,
        ) = stored[layer]
        grad_down_shift = jnp.sum(grad_stream, axis=0)
        branch_grad = core_gather(grad_stream.astype(bf16))
        grad_down = [dot(branch_grad, active[:, z * 768 : z * 768 + 768], 0, 0).astype(bf16) for z in range(2)]
        grad_active = dot(branch_grad, w_down, 1, 0)
        grad_hidden = (grad_active * gelu_slope(hidden)).astype(bf16)
        grad_up_bias = jnp.sum(grad_hidden.astype(f32), axis=0)
        grad_up = [dot(lifted_all, grad_hidden[:, z * 768 : z * 768 + 768], 0, 0).astype(bf16) for z in range(2)]
        down_sum = reduce_stream(place_stream(grad_down), "xyz")
        up_sum = reduce_stream(place_stream(grad_up), "yzx")
        grad_lifted = core_scatter(dot(grad_hidden, w_up, 1, 1))
        grad_low_two, grad_gain_two, grad_shift_two = norm_backward(
            grad_lifted, scaled_two, inverse_two, full_gains[layer, 1]
        )
        grad_middle = grad_stream + grad_low_two
        grad_out_shift = jnp.sum(grad_middle, axis=0)
        attn_grad = core_gather(grad_middle.astype(bf16))
        grad_out = [dot(attn_grad, mixture[:, z * 192 : z * 192 + 192], 0, 0) for z in range(2)]
        grad_mixture = dot(attn_grad, w_out, 1, 0).astype(bf16)
        grad_queries, grad_keys, grad_values = attend_back(
            heads(queries), heads(key_rows), heads(values), log_sum, heads(grad_mixture)
        )
        grad_queries = grad_queries.astype(bf16).reshape(-1, 384)
        grad_pair = jnp.concatenate([grad_keys.reshape(-1, 384), grad_values.reshape(-1, 384)], axis=1)
        own = grad_pair.shape[0] // 2
        grad_pair = (grad_pair[:own] + swap_zl(grad_pair[own:].astype(bf16)).astype(f32)).astype(bf16)
        grad_keys, grad_values = grad_pair[:, :384], grad_pair[:, 384:]
        grad_qkv = [
            jnp.concatenate(
                [part[:, z * 192 : z * 192 + 192] for part in (grad_queries, grad_keys, grad_values)],
                axis=1,
            )
            for z in range(2)
        ]
        grad_in = [dot(normed_all, part, 0, 0) for part in grad_qkv]
        grad_normed = core_scatter(dot(jnp.concatenate(grad_qkv, axis=1), w_qkv, 1, 1))
        grad_low_one, grad_gain_one, grad_shift_one = norm_backward(
            grad_normed, scaled_one, inverse_one, full_gains[layer, 0]
        )
        grad_stream = grad_middle + grad_low_one

        vectors = jnp.stack(
            [
                grad_gain_one,
                grad_gain_two,
                grad_shift_one,
                grad_out_shift,
                grad_shift_two,
                grad_down_shift,
            ]
        )
        vectors = lax.psum(vectors, "core").reshape(6, 32, 2, 2, 6)
        vectors = lax.dynamic_index_in_dim(vectors, core, 3, False).transpose(1, 2, 0, 3)
        bias_sums = jnp.stack(
            [
                jnp.sum(grad_queries.astype(f32), axis=0),
                jnp.sum(grad_values.astype(f32), axis=0),
            ]
        )
        bias_sums = bias_sums.reshape(2, 2, 32, 6).transpose(2, 1, 0, 3)
        up_sums = grad_up_bias.reshape(2, 32, 24).transpose(1, 0, 2)
        vectors = jnp.concatenate(
            [vectors.reshape(32, 2, 36), bias_sums.reshape(32, 2, 12), up_sums], axis=2
        ).reshape(32, 2, 24, 3)
        high, low = split_low(vectors)
        vectors = jnp.pad(jnp.concatenate([high, low], axis=3), ((0, 0), (0, 0), (0, 0), (0, 122)))
        attn_parts = [
            jnp.concatenate(
                [grad_in[z].astype(bf16), grad_out[z].astype(bf16), vectors[:, z].reshape(D, 128)],
                axis=1,
            )
            for z in range(2)
        ]
        attn_sum = reduce_stream(place_stream(attn_parts), "zxy")
        reduced[layer] = (down_sum, up_sum, attn_sum)

    grad_down = jnp.stack([part[0].T for part in reduced])
    grad_up = jnp.stack([part[1] for part in reduced])
    attn = jnp.stack([part[2] for part in reduced])
    grad_in = attn[:, :, :576].reshape(layers, rows, 3, 192).transpose(0, 2, 1, 3)
    grad_out = attn[:, :, 576:768].transpose(0, 2, 1)
    vectors = (attn[:, :, 768:771] + attn[:, :, 771:774]).reshape(layers, 72)
    grad_gains = vectors[:, :12].reshape(layers, 2, 6)
    grad_shifts = vectors[:, 12:36].reshape(layers, 4, 6)
    grad_in_bias = vectors[:, 36:48].reshape(layers, 2, 6)
    grad_up_bias = vectors[:, 48:72]
    return (
        stream,
        grad_stream,
        grad_in,
        grad_in_bias,
        grad_out,
        grad_up,
        grad_up_bias,
        grad_down,
        grad_gains,
        grad_shifts,
    )


def solution(mesh):
    chips = Mesh(mesh.devices.reshape(4, 4, 2, 2, 2), ALL)
    dp, tensor = ("x", "y", "zh"), ("zl", "core")
    both = dp + tensor
    in_specs = (
        P(both, None),
        P(both, None),
        P(None, None, dp, tensor),
        P(None, None, tensor + dp),
        P(None, tensor, dp),
        P(None, dp, tensor),
        P(None, tensor + dp),
        P(None, tensor, dp),
        P(None, None, both),
        P(None, None, both),
    )
    out_specs = (P(both, None), P(both, None)) + in_specs[2:]
    return jax.shard_map(
        per_device, mesh=chips, in_specs=in_specs, out_specs=out_specs, check_vma=False
    )
```

```python
import jax
import jax.numpy as jnp
from jax import lax
from jax.experimental import pallas as pl
from jax.experimental.pallas import tpu as pltpu
from jax.sharding import Mesh, PartitionSpec as P

HEAD_DIM = 64
D = 768
QUERY_ROWS = 512
bf16 = jnp.bfloat16
f32 = jnp.float32

norm_eps = 1e-05
score_scale = 0.125
root_half = 0.7071067811865476
inv_root_two_pi = 0.3989422804014327

CHIPS = ("x", "y", "zh", "zl")
ALL = CHIPS + ("core",)


def norm_forward(stream, gain_row, shift_row):
    row_mean = jnp.mean(stream, axis=-1, keepdims=True)
    centred = stream - row_mean
    variance = jnp.mean(centred * centred, axis=-1, keepdims=True)
    inverse = lax.rsqrt(variance + norm_eps)
    scaled = centred * inverse
    return (scaled * gain_row + shift_row, scaled, inverse)


def norm_backward(grad_output, scaled, inverse, gain_row):
    grad_scaled = grad_output * gain_row
    mean_grad = jnp.mean(grad_scaled, axis=-1, keepdims=True)
    mean_cross = jnp.mean(grad_scaled * scaled, axis=-1, keepdims=True)
    grad_input = inverse * (grad_scaled - mean_grad - scaled * mean_cross)
    return (grad_input, jnp.sum(grad_output * scaled, axis=0), jnp.sum(grad_output, axis=0))


def gelu_slope(hidden):
    normal_cdf = 0.5 * (1.0 + lax.erf(hidden * root_half))
    return normal_cdf + hidden * jnp.exp(-0.5 * hidden * hidden) * inv_root_two_pi


def dot(left, right, left_dim, right_dim):
    return lax.dot_general(
        left, right, (((left_dim,), (right_dim,)), ((), ())), preferred_element_type=f32
    )


def split_low(value):
    high = lax.reduce_precision(value, 8, 7)
    return high.astype(bf16), (value - high).astype(bf16)


def core_gather(value):
    return lax.all_gather(value, "core", axis=0, tiled=True)


def core_scatter(partial):
    rows = partial.shape[0] // 2
    core = lax.axis_index("core")
    away = lax.dynamic_slice_in_dim(partial, (1 - core) * rows, rows, 0).astype(bf16)
    kept = lax.dynamic_slice_in_dim(partial, core * rows, rows, 0)
    return kept + lax.ppermute(away, "core", [(0, 1), (1, 0)]).astype(f32)


def swap_zl(value):
    return lax.ppermute(value, "zl", [(0, 1), (1, 0)])


def tie(value, *others):
    return lax.optimization_barrier((value,) + others)[0]


def swap(value, name, flip):
    count = 4 if name in ("x", "y") else 2
    return lax.ppermute(value, name, [(i, i ^ flip) for i in range(count)])


class Stream:
    def __init__(self, members, order):
        self.members = members
        self.widths = [member.shape[3] // 2 for member in members]
        self.parts = None
        self.todo = [(name, bit) for name in order for bit in ((0,) if name == "z" else (1, 0))]

    def half(self, value, name, bit, mine):
        if name == "z":
            place = lax.axis_index("zl") if mine else 1 - lax.axis_index("zl")
            width = value.shape[3] // 2
            return lax.dynamic_slice_in_dim(value, place * width, width, 3)
        place = lax.axis_index(name.lower())
        dim = "xy".index(name.lower())
        if name in "XY":
            side = (place >> 1) ^ (place & 1) if bit else place >> 1
        else:
            side = (place >> bit) & 1
        side = side if mine else 1 - side
        size = value.shape[dim] // 2
        if name in "XY" and bit:
            pair = [lax.dynamic_slice_in_dim(value, index, 1, dim) for index in (side, 3 - side)]
            return jnp.concatenate(pair, axis=dim)
        return lax.dynamic_slice_in_dim(value, side * size, size, dim)

    def send(self):
        name, bit = self.todo.pop(0)
        if self.parts is None:
            both = [
                jnp.concatenate([self.half(member, name, bit, mine) for member in self.members], axis=3)
                for mine in (False, True)
            ]
            sent, kept = both[0], both[1:]
        else:
            sent = sum(self.half(part, name, bit, False).astype(f32) for part in self.parts)
            kept = [self.half(part, name, bit, True) for part in self.parts]
        if name == "z":
            came = swap(sent.astype(bf16), "zl", 1)
        else:
            came = swap(sent.astype(bf16), name.lower(), 3 if bit != (name in "XY") else 1)
        self.parts = tuple(kept) + (came,)
        if bit == 0:
            self.parts = (sum(part.astype(f32) for part in self.parts).astype(bf16),)


def join(one, other):
    both = Stream([], one.todo and "")
    both.todo = one.todo
    both.widths = one.widths + other.widths
    both.parts = (jnp.concatenate([one.parts[0], other.parts[0]], axis=3),)
    return both


def settle(value, *streams):
    value, parts = lax.optimization_barrier((value, [stream.parts for stream in streams]))
    for stream, part in zip(streams, parts):
        stream.parts = part
    return value


def send(*streams):
    for stream in streams:
        stream.send()


def last_steps(streams):
    low, high = lax.axis_index("zl"), lax.axis_index("zh")
    widths = [width for stream in streams for width in stream.widths]

    def side(place):
        cuts = []
        for stream in streams:
            first = 0
            for width in stream.widths:
                start = first + place * width
                cuts.append(lax.dynamic_slice_in_dim(stream.parts[0][0, 0], start, width, 1))
                first += 2 * width
        return jnp.concatenate(cuts, axis=1)

    came = swap(side(1 - low), "zl", 1)
    kept = side(low).astype(f32) + came.astype(f32)
    return last_step(kept), widths


def last_step(kept):
    high = lax.axis_index("zh")
    rows = kept.shape[0] // 2
    came = swap(lax.dynamic_slice_in_dim(kept, (1 - high) * rows, rows, 0).astype(bf16), "zh", 1)
    return lax.dynamic_slice_in_dim(kept, high * rows, rows, 0) + came.astype(f32)


def split(whole, widths):
    ends = [sum(widths[:index]) for index in range(len(widths) + 1)]
    return [whole[:, first:last] for first, last in zip(ends, ends[1:])]


def sum_direct(value):
    value = jnp.sum(lax.all_to_all(value, ("x", "y"), 0, 0, tiled=True), axis=0)
    rows = value.shape[0] // 2
    high = lax.axis_index("zh")

    def block(k):
        return lax.dynamic_slice_in_dim(value, (high ^ (k >> 1)) * rows, rows, 0)

    return block(0) + sum(
        lax.ppermute(block(k), ("zh", "zl"), [(i, i ^ k) for i in range(4)]) for k in (1, 2, 3)
    )


def as_blocks(value):
    return value.reshape(4, 4, D // 16, value.shape[1])


def narrow_rows():
    row = lax.broadcasted_iota(jnp.int32, (D, D // 4), 0)
    column = lax.broadcasted_iota(jnp.int32, (D, D // 4), 1)
    return ((row // 24 == column // 6) & (row % 24 == column % 6)).astype(f32)


def dims(left, right, left_dim, right_dim, precision=None):
    return lax.dot_general(
        left,
        right,
        (((left_dim,), (right_dim,)), ((), ())),
        preferred_element_type=f32,
        precision=precision,
    )


def one_head(value, head):
    lane = lax.broadcasted_iota(jnp.int32, value.shape, 1)
    return jnp.where((lane >= HEAD_DIM) == (head == 1), value, jnp.zeros_like(value))


def both_heads(first, second):
    place = lax.broadcasted_iota(jnp.int32, first.shape, 0)
    return jnp.where(place < HEAD_DIM, first, second).T


def attend_kernel(q_ref, k_ref, v_ref, mix_ref, lse_ref):
    k, v = k_ref[...], v_ref[...]
    for start in range(0, q_ref.shape[0], QUERY_ROWS):
        rows = slice(start, start + QUERY_ROWS)
        q = q_ref[rows] * jnp.asarray(score_scale, bf16)
        mixed = []
        for head in range(2):
            scores = dims(k, one_head(q, head), 1, 1)
            top = jnp.max(scores, axis=0, keepdims=True)
            weight = jnp.exp(scores - top)
            total = jnp.sum(weight, axis=0, keepdims=True)
            mixed.append(dims(v, weight.astype(bf16), 0, 0) * (1.0 / total))
            lse_ref[0, head : head + 1, rows] = top + jnp.log(total)
        mix_ref[rows] = both_heads(*mixed).astype(bf16)


def attend_back_kernel(q_ref, k_ref, v_ref, lse_ref, mix_ref, dmix_ref, dq_ref, dk_ref, dv_ref):
    k, v = k_ref[...], v_ref[...]
    dk = jnp.zeros(k.shape, f32)
    dv = jnp.zeros(v.shape, f32)
    for start in range(0, q_ref.shape[0], QUERY_ROWS):
        rows = slice(start, start + QUERY_ROWS)
        q = q_ref[rows] * jnp.asarray(score_scale, bf16)
        dmix = dmix_ref[rows]
        product = dmix.astype(f32) * mix_ref[rows].astype(f32)
        lane = lax.broadcasted_iota(jnp.int32, (8, product.shape[1]), 1)
        place = lax.broadcasted_iota(jnp.int32, (8, product.shape[1]), 0)
        chosen = jnp.where((lane >= HEAD_DIM) == (place == 1), 1.0, 0.0)
        delta = dims(chosen, product, 1, 1, lax.Precision.HIGHEST)
        dq = []
        for head in range(2):
            q_head, dmix_head = one_head(q, head), one_head(dmix, head)
            weight = jnp.exp(dims(k, q_head, 1, 1) - lse_ref[0, head : head + 1, rows])
            grad_weight = dims(v, dmix_head, 1, 1)
            grad_scores = (weight * (grad_weight - delta[head : head + 1])).astype(bf16)
            dv += dims(weight.astype(bf16), dmix_head, 1, 0)
            dk += dims(grad_scores, q_head, 1, 0)
            dq.append(dims(k, grad_scores, 0, 0) * score_scale)
        dq_ref[rows] = both_heads(*dq).astype(bf16)
    dk_ref[...] = dk.astype(bf16)
    dv_ref[...] = dv.astype(bf16)


def attend(queries, pair):
    rows, keys = queries.shape[0], pair.shape[0]
    count = queries.shape[1] // 128
    return pl.pallas_call(
        attend_kernel,
        grid=(count,),
        in_specs=[
            pl.BlockSpec((rows, 128), lambda i: (0, i)),
            pl.BlockSpec((keys, 128), lambda i: (0, i)),
            pl.BlockSpec((keys, 128), lambda i: (0, i + count)),
        ],
        out_specs=[
            pl.BlockSpec((rows, 128), lambda i: (0, i)),
            pl.BlockSpec((1, 8, rows), lambda i: (i, 0, 0)),
        ],
        out_shape=[
            jax.ShapeDtypeStruct(queries.shape, bf16),
            jax.ShapeDtypeStruct((count, 8, rows), f32),
        ],
        compiler_params=pltpu.CompilerParams(vmem_limit_bytes=40 * 2**20),
    )(queries, pair, pair)


def attend_back(queries, pair, log_sum, mixture, grad_mixture):
    rows, keys = queries.shape[0], pair.shape[0]
    count = queries.shape[1] // 128
    narrow = pl.BlockSpec((rows, 128), lambda i: (0, i))
    key_block = pl.BlockSpec((keys, 128), lambda i: (0, i))
    return pl.pallas_call(
        attend_back_kernel,
        grid=(count,),
        in_specs=[
            narrow,
            key_block,
            pl.BlockSpec((keys, 128), lambda i: (0, i + count)),
            pl.BlockSpec((1, 8, rows), lambda i: (i, 0, 0)),
            narrow,
            narrow,
        ],
        out_specs=[narrow, key_block, key_block],
        out_shape=[
            jax.ShapeDtypeStruct(queries.shape, bf16),
            jax.ShapeDtypeStruct((keys, queries.shape[1]), bf16),
            jax.ShapeDtypeStruct((keys, queries.shape[1]), bf16),
        ],
        compiler_params=pltpu.CompilerParams(vmem_limit_bytes=40 * 2**20),
    )(queries, pair, pair, log_sum, mixture, grad_mixture)


def per_device(
    input_frames,
    cotangent,
    attention_in,
    attention_bias,
    attention_out,
    up_weight,
    up_bias,
    down_weight,
    norm_gains,
    row_shifts,
):
    layers = attention_in.shape[0]
    core = lax.axis_index("core")
    rows = D // 32

    own_place = (2 * lax.axis_index("zl") + core) * 6
    vectors = jnp.concatenate([norm_gains.reshape(4, 6), row_shifts.reshape(8, 6)], axis=0).T
    vectors = lax.dynamic_update_slice(jnp.zeros((rows, 12), f32), vectors, (own_place, 0))
    vectors = lax.all_gather(vectors, "core", axis=0)
    high, low = split_low(vectors[0] + vectors[1])
    in_bias = jnp.pad(attention_bias.reshape(4, 6).T, ((0, 18), (0, 0)))
    small = jnp.concatenate([high, low, in_bias, up_bias.T], axis=1)
    small = jnp.pad(small, ((0, 0), (0, 98)))

    def packed(layer):
        return jnp.concatenate(
            [
                down_weight[layer].T,
                up_weight[layer],
                attention_in[layer, 0],
                attention_in[layer, 1],
                attention_in[layer, 2],
                attention_out[layer].T,
            ],
            axis=1,
        )

    frames_all = jnp.concatenate([core_gather(input_frames), core_gather(swap_zl(input_frames))], axis=0)
    gathered = []
    for layer in range(layers):
        block = packed(layer)
        if layer == 0:
            block = jnp.concatenate([block, small], axis=1)
        else:
            block = tie(block, whole)
        whole = lax.all_gather(block, CHIPS, axis=0, tiled=True)
        if layer == 0:
            whole, frames_all = lax.optimization_barrier((whole, frames_all))
        gathered.append(whole.reshape(32, 2, rows, block.shape[1]))

    def columns(layer, first, last):
        halves = [gathered[layer][:, z, :, first:last].reshape(D, last - first) for z in range(2)]
        return jnp.concatenate(halves, axis=1)

    tiny = [gathered[0][:, z, :, 2304:2432].reshape(D, 128).astype(f32).T for z in range(2)]
    full = tiny[0] + tiny[1]
    full = full[:12] + full[12:24]
    full_gains = full[:4].reshape(2, 2, D)
    full_shifts = full[4:].reshape(2, 4, D)
    in_bias = jnp.concatenate([dot(part[24:32], narrow_rows(), 1, 0)[:4] for part in tiny], axis=1)
    in_bias = in_bias.reshape(2, 2, 384)
    hidden_bias = jnp.concatenate([part[28:30] for part in tiny], axis=1)

    def weights_of(layer):
        cuts = ((1536, 1728), (1728, 1920), (1920, 2112))
        w_q, w_k, w_v = [columns(layer, first, last) for first, last in cuts]
        w_kv = jnp.concatenate([w_k, w_v], axis=1)
        return (
            columns(layer, 0, 768),
            columns(layer, 768, 1536),
            w_q,
            w_kv,
            columns(layer, 2112, 2304),
        )

    stream = input_frames.astype(f32)
    stored = []
    for layer in range(layers):
        weights = weights_of(layer)
        w_down, w_up, w_q, w_kv, w_out = weights
        q_bias = in_bias[layer, 0]
        kv_bias = jnp.concatenate([jnp.zeros((384,), f32), in_bias[layer, 1]])
        gain, shift = full_gains[layer, 0], full_shifts[layer, 0]
        normed, scaled_one, inverse_one = norm_forward(stream, gain, shift)
        if layer == 0:
            normed_all = norm_forward(frames_all.astype(f32), gain, shift)[0].astype(bf16)
        else:
            normed = normed.astype(bf16)
            normed_all = jnp.concatenate([core_gather(normed), core_gather(swap_zl(normed))], axis=0)
        own = normed_all.shape[0] // 2
        queries = (dot(normed_all[:own], w_q, 1, 0) + q_bias).astype(bf16)
        pair = (dot(normed_all, w_kv, 1, 0) + kv_bias).astype(bf16)
        mixture, log_sum = attend(queries, pair)
        middle = stream + core_scatter(dot(mixture, w_out, 1, 1)) + full_shifts[layer, 1]
        lifted, scaled_two, inverse_two = norm_forward(
            middle, full_gains[layer, 1], full_shifts[layer, 2]
        )
        lifted_all = core_gather(lifted.astype(bf16))
        hidden = dot(lifted_all, w_up, 1, 0) + hidden_bias[layer]
        active = jax.nn.gelu(hidden, approximate=False).astype(bf16)
        stream = middle + core_scatter(dot(active, w_down, 1, 1)) + full_shifts[layer, 3]
        stored.append(
            (
                weights,
                normed_all,
                scaled_one,
                inverse_one,
                queries,
                pair,
                log_sum,
                mixture,
                scaled_two,
                inverse_two,
                lifted_all,
                hidden,
                active,
            )
        )

    grad_stream = cotangent.astype(f32)
    later = []
    vectors, up_sums, in_sums = [], [], []
    for layer in reversed(range(layers)):
        (
            (w_down, w_up, w_q, w_kv, w_out),
            normed_all,
            scaled_one,
            inverse_one,
            queries,
            pair,
            log_sum,
            mixture,
            scaled_two,
            inverse_two,
            lifted_all,
            hidden,
            active,
        ) = stored[layer]
        own = normed_all.shape[0] // 2
        grad_down_shift = jnp.sum(grad_stream, axis=0)
        branch_grad = core_gather(grad_stream.astype(bf16))
        if later:
            branch_grad = settle(branch_grad, *later[:2])
            send(*later[:2])
        grad_down = as_blocks(dot(branch_grad, active, 0, 0).astype(bf16))
        grad_active = dot(branch_grad, w_down, 1, 0)
        grad_hidden = (grad_active * gelu_slope(hidden)).astype(bf16)
        grad_up_bias = jnp.sum(grad_hidden.astype(f32), axis=0)
        grad_up = as_blocks(dot(lifted_all, grad_hidden, 0, 0).astype(bf16))
        streams = [
            Stream([grad_down], "xy"),
            Stream([grad_up], "yx"),
        ]
        if later:
            grad_hidden = settle(grad_hidden, *later[:2])
            send(*later[:2])
        send(*streams)
        grad_lifted = core_scatter(dot(grad_hidden, w_up, 1, 1))
        grad_low_two, grad_gain_two, grad_shift_two = norm_backward(
            grad_lifted, scaled_two, inverse_two, full_gains[layer, 1]
        )
        grad_middle = grad_stream + grad_low_two
        grad_out_shift = jnp.sum(grad_middle, axis=0)
        attn_grad = core_gather(grad_middle.astype(bf16))
        grad_out = dot(attn_grad, mixture, 0, 0).astype(bf16)
        grad_mixture = dot(attn_grad, w_out, 1, 0).astype(bf16)
        if later:
            grad_mixture = settle(grad_mixture, later[2])
            send(later[2])
        grad_queries, grad_keys, grad_values = attend_back(
            queries, pair, log_sum, mixture, grad_mixture
        )
        grad_pair = jnp.concatenate([grad_keys, grad_values], axis=1)
        grad_pair = settle(grad_pair, *streams, *later)
        send(*streams)
        if later:
            send(later[2])
        away = swap_zl(core_scatter(dot(grad_pair[own:], w_kv, 1, 1)).astype(bf16))
        grad_in_q = dot(normed_all[:own], grad_queries, 0, 0).astype(bf16)
        grad_in_kv = dot(normed_all, grad_pair, 0, 0).astype(bf16)
        grad_normed = core_scatter(
            dot(grad_queries, w_q, 1, 1) + dot(grad_pair[:own], w_kv, 1, 1)
        ) + away.astype(f32)
        grad_low_one, grad_gain_one, grad_shift_one = norm_backward(
            grad_normed, scaled_one, inverse_one, full_gains[layer, 0]
        )
        grad_stream = grad_middle + grad_low_one

        bias_sums = jnp.stack(
            [
                jnp.sum(grad_queries.astype(f32), axis=0),
                jnp.sum(grad_pair[:, 384:].astype(f32), axis=0),
            ]
        )
        vectors.append(
            [
                grad_gain_one,
                grad_gain_two,
                grad_shift_one,
                grad_out_shift,
                grad_shift_two,
                grad_down_shift,
            ]
        )
        up_sums.append(grad_up_bias)
        in_sums.append(bias_sums)
        grad_in_q = tie(grad_in_q, away)
        parts = [grad_in_q, grad_in_kv[:, :384], grad_in_kv[:, 384:], grad_out]
        part_q, part_k, part_v, part_o = [as_blocks(part) for part in parts]
        if layer > 0:
            attn = [Stream([part_q, part_k, part_v, part_o], "zXY")]
            send(*attn)
            later = streams + attn
        else:
            attn = [Stream([part_q, part_o], "xy"), Stream([part_k, part_v], "yx")]
            send(*attn)
            streams += attn
            grad_stream = settle(grad_stream, *streams, *later)

    spread = [
        lax.dot_general(
            jnp.concatenate([sums[:, z * 192 : z * 192 + 192] for sums in in_sums]),
            narrow_rows(),
            (((1,), (1,)), ((), ())),
            precision=lax.Precision.HIGHEST,
            preferred_element_type=f32,
        )
        for z in range(2)
    ]
    shared = jnp.stack(vectors[0] + vectors[1])
    both = [
        jnp.pad(
            jnp.concatenate(
                [shared, spread[z], jnp.stack([sums[z * D : z * D + D] for sums in up_sums])]
            ),
            ((0, 46), (0, 0)),
        )
        for z in range(2)
    ]
    small = sum_direct(jnp.concatenate(both).T.reshape(16, D // 16, 128))
    small = lax.dynamic_slice_in_dim(small, lax.axis_index("zl") * 64, 64, 1)
    send(streams[2], streams[3], later[2])
    small = settle(small, streams[2], streams[3], later[2])
    streams = [join(streams[0], streams[2]), join(streams[1], streams[3])]
    send(*streams, later[2])
    grad_stream = settle(grad_stream, *streams, later[2])
    send(*streams)
    last, widths = last_steps(streams)
    down_0, q_0, o_0, up_0, k_0, v_0 = split(last, widths)
    last, widths = last_steps(later[:2])
    down_1, up_1 = split(last, widths)
    last = last_step(later[2].parts[0][0, 0].astype(f32))
    q_1, k_1, v_1, o_1 = split(last, later[2].widths)
    shared = lax.dynamic_slice_in_dim(lax.psum(small[:, :12], "core"), own_place, 6, 0).T
    shared = shared.reshape(2, 6, 6)[::-1]
    grad_gains = shared[:, :2]
    grad_shifts = shared[:, 2:]
    grad_in_bias = small[:6, 12:16].T.reshape(2, 2, 6)[::-1]
    grad_up_bias = small[:, 16:18].T[::-1]

    grad_down = jnp.stack([down_0.T, down_1.T])
    grad_up = jnp.stack([up_0, up_1])
    grad_in = jnp.stack([q_0, k_0, v_0, q_1, k_1, v_1])
    grad_in = grad_in.reshape(layers, 3, rows, 192)
    grad_out = jnp.stack([o_0.T, o_1.T])
    return (
        stream,
        grad_stream,
        grad_in,
        grad_in_bias,
        grad_out,
        grad_up,
        grad_up_bias,
        grad_down,
        grad_gains,
        grad_shifts,
    )


def solution(mesh):
    chips = Mesh(mesh.devices.reshape(4, 4, 2, 2, 2), ALL)
    dp, tensor = ("x", "y", "zh"), ("zl", "core")
    both = dp + tensor
    in_specs = (
        P(both, None),
        P(both, None),
        P(None, None, dp, tensor),
        P(None, None, tensor + dp),
        P(None, tensor, dp),
        P(None, dp, tensor),
        P(None, tensor + dp),
        P(None, tensor, dp),
        P(None, None, both),
        P(None, None, both),
    )
    out_specs = (P(both, None), P(both, None)) + in_specs[2:]
    return jax.shard_map(
        per_device, mesh=chips, in_specs=in_specs, out_specs=out_specs, check_vma=False
    )
```

```python
import jax
import jax.numpy as jnp
from jax import lax
from jax.experimental import pallas as pl
from jax.experimental.pallas import tpu as pltpu
from jax.sharding import Mesh, PartitionSpec as P

HEAD_DIM = 64
D = 768
QUERY_ROWS = 512
bf16 = jnp.bfloat16
f32 = jnp.float32

norm_eps = 1e-05
score_scale = 0.125
root_half = 0.7071067811865476
inv_root_two_pi = 0.3989422804014327

CHIPS = ("x", "y", "zh", "zl")
ALL = CHIPS + ("core",)


def norm_forward(stream, gain_row, shift_row):
    row_mean = jnp.mean(stream, axis=-1, keepdims=True)
    centred = stream - row_mean
    variance = jnp.mean(centred * centred, axis=-1, keepdims=True)
    inverse = lax.rsqrt(variance + norm_eps)
    scaled = centred * inverse
    return (scaled * gain_row + shift_row, scaled, inverse)


def norm_backward(grad_output, scaled, inverse, gain_row):
    grad_scaled = grad_output * gain_row
    mean_grad = jnp.mean(grad_scaled, axis=-1, keepdims=True)
    mean_cross = jnp.mean(grad_scaled * scaled, axis=-1, keepdims=True)
    grad_input = inverse * (grad_scaled - mean_grad - scaled * mean_cross)
    return (grad_input, jnp.sum(grad_output * scaled, axis=0), jnp.sum(grad_output, axis=0))


def gelu_slope(hidden):
    normal_cdf = 0.5 * (1.0 + lax.erf(hidden * root_half))
    return normal_cdf + hidden * jnp.exp(-0.5 * hidden * hidden) * inv_root_two_pi


def dot(left, right, left_dim, right_dim):
    return lax.dot_general(
        left, right, (((left_dim,), (right_dim,)), ((), ())), preferred_element_type=f32
    )


def split_low(value):
    high = lax.reduce_precision(value, 8, 7)
    return high.astype(bf16), (value - high).astype(bf16)


def core_gather(value):
    return lax.all_gather(value, "core", axis=0, tiled=True)


def core_scatter(partial):
    rows = partial.shape[0] // 2
    core = lax.axis_index("core")
    away = lax.dynamic_slice_in_dim(partial, (1 - core) * rows, rows, 0).astype(bf16)
    kept = lax.dynamic_slice_in_dim(partial, core * rows, rows, 0)
    return kept + lax.ppermute(away, "core", [(0, 1), (1, 0)]).astype(f32)


def swap_zl(value):
    return lax.ppermute(value, "zl", [(0, 1), (1, 0)])


def tie(value, *others):
    return lax.optimization_barrier((value,) + others)[0]


def swap(value, name, flip):
    count = 4 if name in ("x", "y") else 2
    return lax.ppermute(value, name, [(i, i ^ flip) for i in range(count)])


class Stream:
    def __init__(self, members, order):
        self.members = members
        self.widths = [member.shape[3] // 2 for member in members]
        self.single = [order[0] == "z" for _ in members]
        self.parts = None
        self.todo = [(name, bit) for name in order for bit in ((0,) if name == "z" else (1, 0))]

    def half(self, value, name, bit, mine):
        if name == "z":
            place = lax.axis_index("zl") if mine else 1 - lax.axis_index("zl")
            width = value.shape[3] // 2
            return lax.dynamic_slice_in_dim(value, place * width, width, 3)
        place = lax.axis_index(name.lower())
        dim = "xy".index(name.lower())
        if name in "XY":
            side = (place >> 1) ^ (place & 1) if bit else place >> 1
        else:
            side = (place >> bit) & 1
        side = side if mine else 1 - side
        size = value.shape[dim] // 2
        if name in "XY" and bit:
            pair = [lax.dynamic_slice_in_dim(value, index, 1, dim) for index in (side, 3 - side)]
            return jnp.concatenate(pair, axis=dim)
        return lax.dynamic_slice_in_dim(value, side * size, size, dim)

    def send(self):
        name, bit = self.todo.pop(0)
        if self.parts is None:
            both = [
                jnp.concatenate([self.half(member, name, bit, mine) for member in self.members], axis=3)
                for mine in (False, True)
            ]
            sent, kept = both[0], both[1:]
        else:
            sent = sum(self.half(part, name, bit, False).astype(f32) for part in self.parts)
            kept = [self.half(part, name, bit, True) for part in self.parts]
        if name == "z":
            came = swap(sent.astype(bf16), "zl", 1)
        else:
            came = swap(sent.astype(bf16), name.lower(), 3 if bit != (name in "XY") else 1)
        self.parts = tuple(kept) + (came,)
        if bit == 0:
            self.parts = (sum(part.astype(f32) for part in self.parts).astype(bf16),)


def join(*streams):
    whole = Stream([], "")
    whole.todo = streams[0].todo
    whole.widths = [width for stream in streams for width in stream.widths]
    whole.single = [single for stream in streams for single in stream.single]
    whole.parts = (jnp.concatenate([stream.parts[0] for stream in streams], axis=3),)
    return whole


def settle(value, *streams):
    value, parts = lax.optimization_barrier((value, [stream.parts for stream in streams]))
    for stream, part in zip(streams, parts):
        stream.parts = part
    return value


def send(*streams):
    for stream in streams:
        stream.send()


def last_step(streams):
    low, high = lax.axis_index("zl"), lax.axis_index("zh")

    def block(k, singles):
        cuts = []
        for stream in streams:
            first = 0
            for width, single in zip(stream.widths, stream.single):
                if single == singles:
                    start = first if single else first + (low ^ (k & 1)) * width
                    cuts.append(lax.dynamic_slice_in_dim(stream.parts[0][0, 0], start, width, 1))
                first += width if single else 2 * width
        whole = jnp.concatenate(cuts, axis=1)
        rows = whole.shape[0] // 2
        return lax.dynamic_slice_in_dim(whole, (high ^ (k >> 1)) * rows, rows, 0)

    def message(k):
        return jnp.concatenate([block(k, False), block(k, True)], axis=1) if k in (0, 2) else block(k, False)

    came = [
        lax.ppermute(message(k), ("zh", "zl"), [(i, i ^ k) for i in range(4)]).astype(f32)
        for k in (1, 2, 3)
    ]
    total = message(0).astype(f32) + came[1]
    shared = came[0].shape[1]
    total = jnp.concatenate([total[:, :shared] + came[0] + came[2], total[:, shared:]], axis=1)
    pairs = [w for stream in streams for w, single in zip(stream.widths, stream.single) if not single]
    singles = [w for stream in streams for w, single in zip(stream.widths, stream.single) if single]
    return split(total, pairs + singles)


def split(whole, widths):
    ends = [sum(widths[:index]) for index in range(len(widths) + 1)]
    return [whole[:, first:last] for first, last in zip(ends, ends[1:])]


def sum_direct(value):
    rows = value.shape[0] // 2
    high = lax.axis_index("zh")

    def block(k):
        return lax.dynamic_slice_in_dim(value, (high ^ (k >> 1)) * rows, rows, 0)

    return block(0) + sum(
        lax.ppermute(block(k), ("zh", "zl"), [(i, i ^ k) for i in range(4)]) for k in (1, 2, 3)
    )


def as_blocks(value):
    return value.reshape(4, 4, D // 16, value.shape[1])


def narrow_rows():
    row = lax.broadcasted_iota(jnp.int32, (D, D // 4), 0)
    column = lax.broadcasted_iota(jnp.int32, (D, D // 4), 1)
    return ((row // 24 == column // 6) & (row % 24 == column % 6)).astype(f32)


def dims(left, right, left_dim, right_dim, precision=None):
    return lax.dot_general(
        left,
        right,
        (((left_dim,), (right_dim,)), ((), ())),
        preferred_element_type=f32,
        precision=precision,
    )


def one_head(value, head):
    lane = lax.broadcasted_iota(jnp.int32, value.shape, 1)
    return jnp.where((lane >= HEAD_DIM) == (head == 1), value, jnp.zeros_like(value))


def both_heads(first, second):
    place = lax.broadcasted_iota(jnp.int32, first.shape, 0)
    return jnp.where(place < HEAD_DIM, first, second).T


def attend_kernel(q_ref, k_ref, v_ref, mix_ref, lse_ref):
    k, v = k_ref[...], v_ref[...]
    for start in range(0, q_ref.shape[0], QUERY_ROWS):
        rows = slice(start, start + QUERY_ROWS)
        q = q_ref[rows] * jnp.asarray(score_scale, bf16)
        mixed = []
        for head in range(2):
            scores = dims(k, one_head(q, head), 1, 1)
            top = jnp.max(scores, axis=0, keepdims=True)
            weight = jnp.exp(scores - top)
            total = jnp.sum(weight, axis=0, keepdims=True)
            mixed.append(dims(v, weight.astype(bf16), 0, 0) * (1.0 / total))
            lse_ref[0, head : head + 1, rows] = top + jnp.log(total)
        mix_ref[rows] = both_heads(*mixed).astype(bf16)


def attend_back_kernel(q_ref, k_ref, v_ref, lse_ref, mix_ref, dmix_ref, dq_ref, dk_ref, dv_ref):
    k, v = k_ref[...], v_ref[...]
    dk = jnp.zeros(k.shape, f32)
    dv = jnp.zeros(v.shape, f32)
    for start in range(0, q_ref.shape[0], QUERY_ROWS):
        rows = slice(start, start + QUERY_ROWS)
        q = q_ref[rows] * jnp.asarray(score_scale, bf16)
        dmix = dmix_ref[rows]
        product = dmix.astype(f32) * mix_ref[rows].astype(f32)
        lane = lax.broadcasted_iota(jnp.int32, (8, product.shape[1]), 1)
        place = lax.broadcasted_iota(jnp.int32, (8, product.shape[1]), 0)
        chosen = jnp.where((lane >= HEAD_DIM) == (place == 1), 1.0, 0.0)
        delta = dims(chosen, product, 1, 1, lax.Precision.HIGHEST)
        dq = []
        for head in range(2):
            q_head, dmix_head = one_head(q, head), one_head(dmix, head)
            weight = jnp.exp(dims(k, q_head, 1, 1) - lse_ref[0, head : head + 1, rows])
            grad_weight = dims(v, dmix_head, 1, 1)
            grad_scores = (weight * (grad_weight - delta[head : head + 1])).astype(bf16)
            dv += dims(weight.astype(bf16), dmix_head, 1, 0)
            dk += dims(grad_scores, q_head, 1, 0)
            dq.append(dims(k, grad_scores, 0, 0) * score_scale)
        dq_ref[rows] = both_heads(*dq).astype(bf16)
    dk_ref[...] = dk.astype(bf16)
    dv_ref[...] = dv.astype(bf16)


def attend(queries, pair):
    rows, keys = queries.shape[0], pair.shape[0]
    count = queries.shape[1] // 128
    return pl.pallas_call(
        attend_kernel,
        grid=(count,),
        in_specs=[
            pl.BlockSpec((rows, 128), lambda i: (0, i)),
            pl.BlockSpec((keys, 128), lambda i: (0, i)),
            pl.BlockSpec((keys, 128), lambda i: (0, i + count)),
        ],
        out_specs=[
            pl.BlockSpec((rows, 128), lambda i: (0, i)),
            pl.BlockSpec((1, 8, rows), lambda i: (i, 0, 0)),
        ],
        out_shape=[
            jax.ShapeDtypeStruct(queries.shape, bf16),
            jax.ShapeDtypeStruct((count, 8, rows), f32),
        ],
        compiler_params=pltpu.CompilerParams(vmem_limit_bytes=40 * 2**20),
        cost_estimate=pl.CostEstimate(
            flops=16 * HEAD_DIM * count * rows * keys,
            bytes_accessed=4 * queries.size + 2 * pair.size,
            transcendentals=2 * count * rows * keys,
        ),
    )(queries, pair, pair)


def attend_back(queries, pair, log_sum, mixture, grad_mixture):
    rows, keys = queries.shape[0], pair.shape[0]
    count = queries.shape[1] // 128
    narrow = pl.BlockSpec((rows, 128), lambda i: (0, i))
    key_block = pl.BlockSpec((keys, 128), lambda i: (0, i))
    return pl.pallas_call(
        attend_back_kernel,
        grid=(count,),
        in_specs=[
            narrow,
            key_block,
            pl.BlockSpec((keys, 128), lambda i: (0, i + count)),
            pl.BlockSpec((1, 8, rows), lambda i: (i, 0, 0)),
            narrow,
            narrow,
        ],
        out_specs=[narrow, key_block, key_block],
        out_shape=[
            jax.ShapeDtypeStruct(queries.shape, bf16),
            jax.ShapeDtypeStruct((keys, queries.shape[1]), bf16),
            jax.ShapeDtypeStruct((keys, queries.shape[1]), bf16),
        ],
        compiler_params=pltpu.CompilerParams(vmem_limit_bytes=40 * 2**20),
        cost_estimate=pl.CostEstimate(
            flops=40 * HEAD_DIM * count * rows * keys,
            bytes_accessed=8 * queries.size + 4 * pair.size,
            transcendentals=2 * count * rows * keys,
        ),
    )(queries, pair, pair, log_sum, mixture, grad_mixture)


def per_device(
    input_frames,
    cotangent,
    attention_in,
    attention_bias,
    attention_out,
    up_weight,
    up_bias,
    down_weight,
    norm_gains,
    row_shifts,
):
    layers = attention_in.shape[0]
    core = lax.axis_index("core")
    rows = D // 32

    own_place = (2 * lax.axis_index("zl") + core) * 6
    vectors = jnp.concatenate([norm_gains.reshape(4, 6), row_shifts.reshape(8, 6)], axis=0).T
    vectors = lax.dynamic_update_slice(jnp.zeros((rows, 12), f32), vectors, (own_place, 0))
    vectors = lax.all_gather(vectors, "core", axis=0)
    high, low = split_low(vectors[0] + vectors[1])
    in_bias = jnp.pad(attention_bias.reshape(4, 6).T, ((0, 18), (0, 0)))
    small = jnp.concatenate([high, low, in_bias, up_bias.T], axis=1)
    small = jnp.pad(small, ((0, 0), (0, 98)))

    def packed(layer):
        return jnp.concatenate(
            [
                down_weight[layer].T,
                up_weight[layer],
                attention_in[layer, 0],
                attention_in[layer, 1],
                attention_in[layer, 2],
                attention_out[layer].T,
            ],
            axis=1,
        )

    frames_all = jnp.concatenate([core_gather(input_frames), core_gather(swap_zl(input_frames))], axis=0)
    blocks = [packed(layer) for layer in range(layers)]
    first = lax.all_gather(
        jnp.concatenate([blocks[0], blocks[1][:, 1536:], small], axis=1), CHIPS, axis=0, tiled=True
    )
    first, frames_all, cotangent_all = lax.optimization_barrier(
        (first, frames_all, core_gather(cotangent))
    )
    second = lax.all_gather(tie(blocks[1][:, :1536], first), CHIPS, axis=0, tiled=True)
    first = first.reshape(32, 2, rows, 3200)
    second = second.reshape(32, 2, rows, 1536)

    def columns(layer, start, end):
        if layer == 0:
            source = first
        elif end <= 1536:
            source = second
        else:
            source, start, end = first, start + 768, end + 768
        halves = [source[:, z, :, start:end].reshape(D, end - start) for z in range(2)]
        return jnp.concatenate(halves, axis=1)

    tiny = [first[:, z, :, 3072:3200].reshape(D, 128).astype(f32).T for z in range(2)]
    full = tiny[0] + tiny[1]
    full = full[:12] + full[12:24]
    full_gains = full[:4].reshape(2, 2, D)
    full_shifts = full[4:].reshape(2, 4, D)
    in_bias = jnp.concatenate([dot(part[24:32], narrow_rows(), 1, 0)[:4] for part in tiny], axis=1)
    in_bias = in_bias.reshape(2, 2, 384)
    hidden_bias = jnp.concatenate([part[28:30] for part in tiny], axis=1)

    def weights_of(layer):
        cuts = ((1536, 1728), (1728, 1920), (1920, 2112))
        w_q, w_k, w_v = [columns(layer, first, last) for first, last in cuts]
        w_kv = jnp.concatenate([w_k, w_v], axis=1)
        return (
            columns(layer, 0, 768),
            columns(layer, 768, 1536),
            w_q,
            w_kv,
            columns(layer, 2112, 2304),
        )

    stream = input_frames.astype(f32)
    stored = []
    for layer in range(layers):
        weights = weights_of(layer)
        w_down, w_up, w_q, w_kv, w_out = weights
        q_bias = in_bias[layer, 0]
        kv_bias = jnp.concatenate([jnp.zeros((384,), f32), in_bias[layer, 1]])
        gain, shift = full_gains[layer, 0], full_shifts[layer, 0]
        normed, scaled_one, inverse_one = norm_forward(stream, gain, shift)
        if layer == 0:
            normed_all = norm_forward(frames_all.astype(f32), gain, shift)[0].astype(bf16)
        else:
            normed = normed.astype(bf16)
            normed_all = jnp.concatenate([core_gather(normed), core_gather(swap_zl(normed))], axis=0)
        own = normed_all.shape[0] // 2
        queries = (dot(normed_all[:own], w_q, 1, 0) + q_bias).astype(bf16)
        pair = (dot(normed_all, w_kv, 1, 0) + kv_bias).astype(bf16)
        mixture, log_sum = attend(queries, pair)
        middle = stream + core_scatter(dot(mixture, w_out, 1, 1)) + full_shifts[layer, 1]
        lifted, scaled_two, inverse_two = norm_forward(
            middle, full_gains[layer, 1], full_shifts[layer, 2]
        )
        lifted_all = core_gather(lifted.astype(bf16))
        hidden = dot(lifted_all, w_up, 1, 0) + hidden_bias[layer]
        active = (0.5 * hidden * (1.0 + lax.erf(hidden * root_half))).astype(bf16)
        stream = middle + core_scatter(dot(active, w_down, 1, 1)) + full_shifts[layer, 3]
        stored.append(
            (
                weights,
                normed_all,
                scaled_one,
                inverse_one,
                queries,
                pair,
                log_sum,
                mixture,
                scaled_two,
                inverse_two,
                lifted_all,
                hidden,
                active,
            )
        )

    grad_stream = cotangent.astype(f32)
    later = []
    vectors, up_sums, in_sums = [], [], []
    for layer in reversed(range(layers)):
        (
            (w_down, w_up, w_q, w_kv, w_out),
            normed_all,
            scaled_one,
            inverse_one,
            queries,
            pair,
            log_sum,
            mixture,
            scaled_two,
            inverse_two,
            lifted_all,
            hidden,
            active,
        ) = stored[layer]
        own = normed_all.shape[0] // 2
        grad_down_shift = jnp.sum(grad_stream, axis=0)
        branch_grad = core_gather(grad_stream.astype(bf16)) if layer < layers - 1 else cotangent_all
        grad_down = as_blocks(dot(branch_grad, active, 0, 0).astype(bf16))
        grad_active = dot(branch_grad, w_down, 1, 0)
        grad_hidden = (grad_active * gelu_slope(hidden)).astype(bf16)
        grad_up_bias = jnp.sum(grad_hidden.astype(f32), axis=0)
        grad_up = as_blocks(dot(lifted_all, grad_hidden, 0, 0).astype(bf16))
        streams = [
            Stream([grad_down], "xy" if layer else "XY"),
            Stream([grad_up], "yx" if layer else "YX"),
        ]
        if later:
            grad_hidden = settle(grad_hidden, *later[:2])
            send(*later[:2])
        send(*streams)
        grad_lifted = core_scatter(dot(grad_hidden, w_up, 1, 1))
        grad_low_two, grad_gain_two, grad_shift_two = norm_backward(
            grad_lifted, scaled_two, inverse_two, full_gains[layer, 1]
        )
        grad_middle = grad_stream + grad_low_two
        grad_out_shift = jnp.sum(grad_middle, axis=0)
        attn_grad = core_gather(grad_middle.astype(bf16))
        grad_out = dot(attn_grad, mixture, 0, 0).astype(bf16)
        grad_mixture = dot(attn_grad, w_out, 1, 0).astype(bf16)
        if later:
            grad_mixture = settle(grad_mixture, *later[:2])
            send(*later[:2])
        grad_queries, grad_keys, grad_values = attend_back(
            queries, pair, log_sum, mixture, grad_mixture
        )
        grad_pair = jnp.concatenate([grad_keys, grad_values], axis=1)
        if later:
            grad_pair = settle(grad_pair, *streams, *later)
            send(*streams, later[2])
        away = core_scatter(dot(grad_pair[own:], w_kv, 1, 1)).astype(bf16)
        if layer > 0:
            away = settle(away, *streams)
            send(*streams)
        away = swap_zl(away)
        grad_in_q = dot(normed_all[:own], grad_queries, 0, 0).astype(bf16)
        grad_in_kv = dot(normed_all, grad_pair, 0, 0).astype(bf16)
        grad_normed = core_scatter(dot(grad_queries, w_q, 1, 1) + dot(grad_pair[:own], w_kv, 1, 1))
        if layer > 0:
            grad_in_q = tie(grad_in_q, away)
        parts = [grad_in_q, grad_in_kv[:, :384], grad_in_kv[:, 384:], grad_out]
        part_q, part_k, part_v, part_o = [as_blocks(part) for part in parts]
        if layer > 0:
            attn = [Stream([part_q, part_k, part_v, part_o], "zXY")]
            send(*attn)
            later = streams + attn
        else:
            attn = [Stream([part_q, part_o], "XY"), Stream([part_k, part_v], "YX")]
            send(*attn)
            grad_normed = settle(grad_normed, *attn, later[2])
            send(*attn, later[2])
        grad_normed = grad_normed + away.astype(f32)
        grad_low_one, grad_gain_one, grad_shift_one = norm_backward(
            grad_normed, scaled_one, inverse_one, full_gains[layer, 0]
        )
        grad_stream = grad_middle + grad_low_one

        bias_sums = jnp.stack(
            [
                jnp.sum(grad_queries.astype(f32), axis=0),
                jnp.sum(grad_pair[:, 384:].astype(f32), axis=0),
            ]
        )
        vectors.append(
            [
                grad_gain_one,
                grad_gain_two,
                grad_shift_one,
                grad_out_shift,
                grad_shift_two,
                grad_down_shift,
            ]
        )
        up_sums.append(grad_up_bias)
        in_sums.append(bias_sums)
    in_sums = settle(jnp.concatenate(in_sums), *streams, *attn, *later)
    streams = [join(streams[0], attn[0], later[2]), join(streams[1], attn[1])]
    send(*streams)
    spread = lax.dot_general(
        jnp.concatenate([in_sums[:, :192], in_sums[:, 192:]]),
        narrow_rows(),
        (((1,), (1,)), ((), ())),
        precision=lax.Precision.HIGHEST,
        preferred_element_type=f32,
    )
    small = [jnp.pad(sums[None], ((0, 7), (0, 0))) for sums in vectors[0] + vectors[1]]
    small.append(spread)
    small += [jnp.pad(sums.reshape(2, D), ((0, 6), (0, 0))) for sums in up_sums]
    small.append(jnp.zeros((8, D), f32))
    small = jnp.concatenate(small).T.reshape(16, D // 16, 128)
    small = jnp.sum(lax.all_to_all(small, ("x", "y"), 0, 0, tiled=True), axis=0)
    send(*streams)
    small = sum_direct(settle(small, *streams))
    pieces = last_step([*streams, *later[:2]])
    down_0, q_0, o_0, up_0, k_0, v_0, down_1, up_1, q_1, k_1, v_1, o_1 = pieces
    side = lax.axis_index("zl")
    shared = lax.psum(small[:, :96].reshape(rows, 12, 8)[:, :, 0], "core")
    shared = lax.dynamic_slice_in_dim(shared, own_place, 6, 0).T.reshape(2, 6, 6)[::-1]
    grad_gains = shared[:, :2]
    grad_shifts = shared[:, 2:]
    grad_in_bias = lax.dynamic_slice(small, (0, 96 + 4 * side), (6, 4)).T.reshape(2, 2, 6)[::-1]
    grad_up_bias = [lax.dynamic_slice_in_dim(small, at + side, 1, 1) for at in (112, 104)]
    grad_up_bias = jnp.concatenate(grad_up_bias, axis=1).T

    grad_down = jnp.stack([down_0.T, down_1.T])
    grad_up = jnp.stack([up_0, up_1])
    grad_in = jnp.stack([q_0, k_0, v_0, q_1, k_1, v_1])
    grad_in = grad_in.reshape(layers, 3, rows, 192)
    grad_out = jnp.stack([o_0.T, o_1.T])
    return (
        stream,
        grad_stream,
        grad_in,
        grad_in_bias,
        grad_out,
        grad_up,
        grad_up_bias,
        grad_down,
        grad_gains,
        grad_shifts,
    )


def solution(mesh):
    chips = Mesh(mesh.devices.reshape(4, 4, 2, 2, 2), ALL)
    dp, tensor = ("x", "y", "zh"), ("zl", "core")
    both = dp + tensor
    in_specs = (
        P(both, None),
        P(both, None),
        P(None, None, dp, tensor),
        P(None, None, tensor + dp),
        P(None, tensor, dp),
        P(None, dp, tensor),
        P(None, tensor + dp),
        P(None, tensor, dp),
        P(None, None, both),
        P(None, None, both),
    )
    out_specs = (P(both, None), P(both, None)) + in_specs[2:]
    return jax.shard_map(
        per_device, mesh=chips, in_specs=in_specs, out_specs=out_specs, check_vma=False
    )
```

```python
import jax
import jax.numpy as jnp
from jax import lax
from jax.experimental import pallas as pl
from jax.experimental.pallas import tpu as pltpu
from jax.sharding import Mesh, PartitionSpec as P

HEAD_DIM = 64
D = 768
QUERY_ROWS = 512
VMEM_BYTES = 20 * 2**20
bf16 = jnp.bfloat16
f32 = jnp.float32

norm_eps = 1e-05
score_scale = 0.125
root_half = 0.7071067811865476
inv_root_two_pi = 0.3989422804014327

CHIPS = ("x", "y", "zh", "zl")
ALL = CHIPS + ("core",)


def norm_forward(stream, gain_row, shift_row):
    row_mean = jnp.mean(stream, axis=-1, keepdims=True)
    centred = stream - row_mean
    variance = jnp.mean(centred * centred, axis=-1, keepdims=True)
    inverse = lax.rsqrt(variance + norm_eps)
    scaled = centred * inverse
    return (scaled * gain_row + shift_row, scaled, inverse)


def norm_backward(grad_output, scaled, inverse, gain_row):
    grad_scaled = grad_output * gain_row
    mean_grad = jnp.mean(grad_scaled, axis=-1, keepdims=True)
    mean_cross = jnp.mean(grad_scaled * scaled, axis=-1, keepdims=True)
    grad_input = inverse * (grad_scaled - mean_grad - scaled * mean_cross)
    return (grad_input, jnp.sum(grad_output * scaled, axis=0), jnp.sum(grad_output, axis=0))


def gelu_slope(hidden):
    normal_cdf = 0.5 * (1.0 + lax.erf(hidden * root_half))
    return normal_cdf + hidden * jnp.exp(-0.5 * hidden * hidden) * inv_root_two_pi


def dot(left, right, left_dim, right_dim):
    return lax.dot_general(
        left, right, (((left_dim,), (right_dim,)), ((), ())), preferred_element_type=f32
    )


def split_low(value):
    high = lax.reduce_precision(value, 8, 7)
    return high.astype(bf16), (value - high).astype(bf16)


def core_gather(value):
    return lax.all_gather(value, "core", axis=0, tiled=True)


def core_scatter(partial):
    rows = partial.shape[0] // 2
    core = lax.axis_index("core")
    away = lax.dynamic_slice_in_dim(partial, (1 - core) * rows, rows, 0).astype(bf16)
    kept = lax.dynamic_slice_in_dim(partial, core * rows, rows, 0)
    return kept + lax.ppermute(away, "core", [(0, 1), (1, 0)]).astype(f32)


def swap_zl(value):
    return lax.ppermute(value, "zl", [(0, 1), (1, 0)])


def tie(value, *others):
    return lax.optimization_barrier((value,) + others)[0]


def swap(value, name, flip):
    count = 4 if name in ("x", "y") else 2
    return lax.ppermute(value, name, [(i, i ^ flip) for i in range(count)])


class Stream:
    def __init__(self, members, order):
        self.members = members
        self.widths = [member.shape[3] // 2 for member in members]
        self.single = [order[0] == "z" for _ in members]
        self.parts = None
        self.todo = [(name, bit) for name in order for bit in ((0,) if name == "z" else (1, 0))]

    def half(self, value, name, bit, mine):
        if name == "z":
            place = lax.axis_index("zl") if mine else 1 - lax.axis_index("zl")
            width = value.shape[3] // 2
            return lax.dynamic_slice_in_dim(value, place * width, width, 3)
        place = lax.axis_index(name.lower())
        dim = "xy".index(name.lower())
        if name in "XY":
            side = (place >> 1) ^ (place & 1) if bit else place >> 1
        else:
            side = (place >> bit) & 1
        side = side if mine else 1 - side
        size = value.shape[dim] // 2
        if name in "XY" and bit:
            pair = [lax.dynamic_slice_in_dim(value, index, 1, dim) for index in (side, 3 - side)]
            return jnp.concatenate(pair, axis=dim)
        return lax.dynamic_slice_in_dim(value, side * size, size, dim)

    def send(self, beside=None):
        name, bit = self.todo.pop(0)
        if self.parts is None:
            both = [
                jnp.concatenate([self.half(member, name, bit, mine) for member in self.members], axis=3)
                for mine in (False, True)
            ]
            sent, kept = both[0], both[1:]
        else:
            sent = sum(self.half(part, name, bit, False).astype(f32) for part in self.parts)
            kept = [self.half(part, name, bit, True) for part in self.parts]
        sent = sent.astype(bf16)
        if beside is not None:
            sent, beside = lax.optimization_barrier((sent, beside))
        if name == "z":
            came = swap(sent, "zl", 1)
        else:
            came = swap(sent, name.lower(), 3 if bit != (name in "XY") else 1)
        self.parts = tuple(kept) + (came,)
        if bit == 0:
            self.parts = (sum(part.astype(f32) for part in self.parts).astype(bf16),)
        return beside


def join(*streams):
    whole = Stream([], "")
    whole.todo = streams[0].todo
    whole.widths = [width for stream in streams for width in stream.widths]
    whole.single = [single for stream in streams for single in stream.single]
    whole.parts = (jnp.concatenate([stream.parts[0] for stream in streams], axis=3),)
    return whole


def settle(value, *streams):
    value, parts = lax.optimization_barrier((value, [stream.parts for stream in streams]))
    for stream, part in zip(streams, parts):
        stream.parts = part
    return value


def send(*streams):
    for stream in streams:
        stream.send()


def last_step(streams):
    low, high = lax.axis_index("zl"), lax.axis_index("zh")

    def block(k, singles):
        cuts = []
        for stream in streams:
            first = 0
            for width, single in zip(stream.widths, stream.single):
                if single == singles:
                    start = first if single else first + (low ^ (k & 1)) * width
                    cuts.append(lax.dynamic_slice_in_dim(stream.parts[0][0, 0], start, width, 1))
                first += width if single else 2 * width
        whole = jnp.concatenate(cuts, axis=1)
        rows = whole.shape[0] // 2
        return lax.dynamic_slice_in_dim(whole, (high ^ (k >> 1)) * rows, rows, 0)

    def message(k):
        return jnp.concatenate([block(k, False), block(k, True)], axis=1) if k in (0, 2) else block(k, False)

    came = [
        lax.ppermute(message(k), ("zh", "zl"), [(i, i ^ k) for i in range(4)]).astype(f32)
        for k in (1, 2, 3)
    ]
    total = message(0).astype(f32) + came[1]
    shared = came[0].shape[1]
    total = jnp.concatenate([total[:, :shared] + came[0] + came[2], total[:, shared:]], axis=1)
    pairs = [w for stream in streams for w, single in zip(stream.widths, stream.single) if not single]
    singles = [w for stream in streams for w, single in zip(stream.widths, stream.single) if single]
    return split(total, pairs + singles)


def split(whole, widths):
    ends = [sum(widths[:index]) for index in range(len(widths) + 1)]
    return [whole[:, first:last] for first, last in zip(ends, ends[1:])]


def sum_direct(value):
    rows = value.shape[0] // 2
    high = lax.axis_index("zh")

    def block(k):
        return lax.dynamic_slice_in_dim(value, (high ^ (k >> 1)) * rows, rows, 0)

    return block(0) + sum(
        lax.ppermute(block(k), ("zh", "zl"), [(i, i ^ k) for i in range(4)]) for k in (1, 2, 3)
    )


def as_blocks(value):
    return value.reshape(4, 4, D // 16, value.shape[1])


def narrow_rows():
    row = lax.broadcasted_iota(jnp.int32, (D, D // 4), 0)
    column = lax.broadcasted_iota(jnp.int32, (D, D // 4), 1)
    return ((row // 24 == column // 6) & (row % 24 == column % 6)).astype(f32)


def dims(left, right, left_dim, right_dim, precision=None):
    return lax.dot_general(
        left,
        right,
        (((left_dim,), (right_dim,)), ((), ())),
        preferred_element_type=f32,
        precision=precision,
    )


def one_head(value, head):
    lane = lax.broadcasted_iota(jnp.int32, value.shape, 1)
    return jnp.where((lane >= HEAD_DIM) == (head == 1), value, jnp.zeros_like(value))


def both_heads(first, second):
    place = lax.broadcasted_iota(jnp.int32, first.shape, 0)
    return jnp.where(place < HEAD_DIM, first, second).T


def attend_kernel(q_ref, k_ref, v_ref, mix_ref, lse_ref):
    k, v = k_ref[...], v_ref[...]
    for start in range(0, q_ref.shape[0], QUERY_ROWS):
        rows = slice(start, start + QUERY_ROWS)
        q = q_ref[rows] * jnp.asarray(score_scale, bf16)
        mixed = []
        for head in range(2):
            scores = dims(k, one_head(q, head), 1, 1)
            top = jnp.max(scores, axis=0, keepdims=True)
            weight = jnp.exp(scores - top)
            total = jnp.sum(weight, axis=0, keepdims=True)
            mixed.append(dims(v, weight.astype(bf16), 0, 0) * (1.0 / total))
            lse_ref[0, head : head + 1, rows] = top + jnp.log(total)
        mix_ref[rows] = both_heads(*mixed).astype(bf16)


def attend_back_kernel(q_ref, k_ref, v_ref, lse_ref, mix_ref, dmix_ref, dq_ref, dk_ref, dv_ref):
    k, v = k_ref[...], v_ref[...]
    dk = jnp.zeros(k.shape, f32)
    dv = jnp.zeros(v.shape, f32)
    for start in range(0, q_ref.shape[0], QUERY_ROWS):
        rows = slice(start, start + QUERY_ROWS)
        q = q_ref[rows] * jnp.asarray(score_scale, bf16)
        dmix = dmix_ref[rows]
        product = dmix.astype(f32) * mix_ref[rows].astype(f32)
        lane = lax.broadcasted_iota(jnp.int32, (8, product.shape[1]), 1)
        place = lax.broadcasted_iota(jnp.int32, (8, product.shape[1]), 0)
        chosen = jnp.where((lane >= HEAD_DIM) == (place == 1), 1.0, 0.0)
        delta = dims(chosen, product, 1, 1, lax.Precision.HIGHEST)
        dq = []
        for head in range(2):
            q_head, dmix_head = one_head(q, head), one_head(dmix, head)
            weight = jnp.exp(dims(k, q_head, 1, 1) - lse_ref[0, head : head + 1, rows])
            grad_weight = dims(v, dmix_head, 1, 1)
            grad_scores = (weight * (grad_weight - delta[head : head + 1])).astype(bf16)
            dv += dims(weight.astype(bf16), dmix_head, 1, 0)
            dk += dims(grad_scores, q_head, 1, 0)
            dq.append(dims(k, grad_scores, 0, 0) * score_scale)
        dq_ref[rows] = both_heads(*dq).astype(bf16)
    dk_ref[...] = dk.astype(bf16)
    dv_ref[...] = dv.astype(bf16)


def attend(queries, pair):
    rows, keys = queries.shape[0], pair.shape[0]
    count = queries.shape[1] // 128
    return pl.pallas_call(
        attend_kernel,
        grid=(count,),
        in_specs=[
            pl.BlockSpec((rows, 128), lambda i: (0, i)),
            pl.BlockSpec((keys, 128), lambda i: (0, i)),
            pl.BlockSpec((keys, 128), lambda i: (0, i + count)),
        ],
        out_specs=[
            pl.BlockSpec((rows, 128), lambda i: (0, i)),
            pl.BlockSpec((1, 8, rows), lambda i: (i, 0, 0)),
        ],
        out_shape=[
            jax.ShapeDtypeStruct(queries.shape, bf16),
            jax.ShapeDtypeStruct((count, 8, rows), f32),
        ],
        compiler_params=pltpu.CompilerParams(vmem_limit_bytes=VMEM_BYTES),
    )(queries, pair, pair)


def attend_back(queries, pair, log_sum, mixture, grad_mixture):
    rows, keys = queries.shape[0], pair.shape[0]
    count = queries.shape[1] // 128
    narrow = pl.BlockSpec((rows, 128), lambda i: (0, i))
    key_block = pl.BlockSpec((keys, 128), lambda i: (0, i))
    return pl.pallas_call(
        attend_back_kernel,
        grid=(count,),
        in_specs=[
            narrow,
            key_block,
            pl.BlockSpec((keys, 128), lambda i: (0, i + count)),
            pl.BlockSpec((1, 8, rows), lambda i: (i, 0, 0)),
            narrow,
            narrow,
        ],
        out_specs=[narrow, key_block, key_block],
        out_shape=[
            jax.ShapeDtypeStruct(queries.shape, bf16),
            jax.ShapeDtypeStruct((keys, queries.shape[1]), bf16),
            jax.ShapeDtypeStruct((keys, queries.shape[1]), bf16),
        ],
        compiler_params=pltpu.CompilerParams(vmem_limit_bytes=VMEM_BYTES),
    )(queries, pair, pair, log_sum, mixture, grad_mixture)


def per_device(
    input_frames,
    cotangent,
    attention_in,
    attention_bias,
    attention_out,
    up_weight,
    up_bias,
    down_weight,
    norm_gains,
    row_shifts,
):
    layers = attention_in.shape[0]
    core = lax.axis_index("core")
    rows = D // 32

    own_place = (2 * lax.axis_index("zl") + core) * 6
    vectors = jnp.concatenate([norm_gains.reshape(4, 6), row_shifts.reshape(8, 6)], axis=0).T
    vectors = lax.dynamic_update_slice(jnp.zeros((rows, 12), f32), vectors, (own_place, 0))
    vectors = lax.all_gather(vectors, "core", axis=0)
    high, low = split_low(vectors[0] + vectors[1])
    in_bias = jnp.pad(attention_bias.reshape(4, 6).T, ((0, 18), (0, 0)))
    small = jnp.concatenate([high, low, in_bias, up_bias.T], axis=1)
    small = jnp.pad(small, ((0, 0), (0, 98)))

    def packed(layer):
        return jnp.concatenate(
            [
                down_weight[layer].T,
                up_weight[layer],
                attention_in[layer, 0],
                attention_in[layer, 1],
                attention_in[layer, 2],
                attention_out[layer].T,
            ],
            axis=1,
        )

    frames_all = jnp.concatenate([core_gather(input_frames), core_gather(swap_zl(input_frames))], axis=0)
    blocks = [packed(layer) for layer in range(layers)]
    first = lax.all_gather(
        jnp.concatenate([blocks[0], blocks[1][:, 1536:], small], axis=1), CHIPS, axis=0, tiled=True
    )
    first, frames_all, cotangent_all = lax.optimization_barrier(
        (first, frames_all, core_gather(cotangent))
    )
    second = lax.all_gather(tie(blocks[1][:, :1536], first), CHIPS, axis=0, tiled=True)
    first = first.reshape(32, 2, rows, 3200)
    second = second.reshape(32, 2, rows, 1536)

    def columns(layer, start, end):
        if layer == 0:
            source = first
        elif end <= 1536:
            source = second
        else:
            source, start, end = first, start + 768, end + 768
        halves = [source[:, z, :, start:end].reshape(D, end - start) for z in range(2)]
        return jnp.concatenate(halves, axis=1)

    tiny = [first[:, z, :, 3072:3200].reshape(D, 128).astype(f32).T for z in range(2)]
    full = tiny[0] + tiny[1]
    full = full[:12] + full[12:24]
    full_gains = full[:4].reshape(2, 2, D)
    full_shifts = full[4:].reshape(2, 4, D)
    in_bias = jnp.concatenate([dot(part[24:32], narrow_rows(), 1, 0)[:4] for part in tiny], axis=1)
    in_bias = in_bias.reshape(2, 2, 384)
    hidden_bias = jnp.concatenate([part[28:30] for part in tiny], axis=1)

    def weights_of(layer):
        cuts = ((1536, 1728), (1728, 1920), (1920, 2112))
        w_q, w_k, w_v = [columns(layer, start, end) for start, end in cuts]
        w_kv = jnp.concatenate([w_k, w_v], axis=1)
        return (
            columns(layer, 0, 768),
            columns(layer, 768, 1536),
            w_q,
            w_kv,
            columns(layer, 2112, 2304),
        )

    stream = input_frames.astype(f32)
    stored = []
    for layer in range(layers):
        if layer > 0:
            first = tie(first, stream)
        weights = weights_of(layer)
        w_down, w_up, w_q, w_kv, w_out = weights
        q_bias = in_bias[layer, 0]
        kv_bias = jnp.concatenate([jnp.zeros((384,), f32), in_bias[layer, 1]])
        gain, shift = full_gains[layer, 0], full_shifts[layer, 0]
        normed, scaled_one, inverse_one = norm_forward(stream, gain, shift)
        if layer == 0:
            normed_all = norm_forward(frames_all.astype(f32), gain, shift)[0].astype(bf16)
        else:
            normed = normed.astype(bf16)
            normed_all = jnp.concatenate([core_gather(normed), core_gather(swap_zl(normed))], axis=0)
        own = normed_all.shape[0] // 2
        queries = (dot(normed_all[:own], w_q, 1, 0) + q_bias).astype(bf16)
        pair = (dot(normed_all, w_kv, 1, 0) + kv_bias).astype(bf16)
        mixture, log_sum = attend(queries, pair)
        middle = stream + core_scatter(dot(mixture, w_out, 1, 1)) + full_shifts[layer, 1]
        lifted, scaled_two, inverse_two = norm_forward(
            middle, full_gains[layer, 1], full_shifts[layer, 2]
        )
        lifted_all = core_gather(lifted.astype(bf16))
        hidden = dot(lifted_all, w_up, 1, 0) + hidden_bias[layer]
        active = (0.5 * hidden * (1.0 + lax.erf(hidden * root_half))).astype(bf16)
        stream = middle + core_scatter(dot(active, w_down, 1, 1)) + full_shifts[layer, 3]
        stored.append(
            (
                weights,
                normed_all,
                scaled_one,
                inverse_one,
                queries,
                pair,
                log_sum,
                mixture,
                scaled_two,
                inverse_two,
                lifted_all,
                hidden,
                active,
            )
        )

    grad_stream = cotangent.astype(f32)
    later = []
    vectors, up_sums, in_sums = [], [], []
    for layer in reversed(range(layers)):
        (
            (w_down, w_up, w_q, w_kv, w_out),
            normed_all,
            scaled_one,
            inverse_one,
            queries,
            pair,
            log_sum,
            mixture,
            scaled_two,
            inverse_two,
            lifted_all,
            hidden,
            active,
        ) = stored[layer]
        own = normed_all.shape[0] // 2
        grad_down_shift = jnp.sum(grad_stream, axis=0)
        branch_grad = core_gather(grad_stream.astype(bf16)) if layer < layers - 1 else cotangent_all
        if later:
            branch_grad = later[2].send(branch_grad)
        grad_down = as_blocks(dot(branch_grad, active, 0, 0).astype(bf16))
        grad_active = dot(branch_grad, w_down, 1, 0)
        grad_hidden = (grad_active * gelu_slope(hidden)).astype(bf16)
        grad_up_bias = jnp.sum(grad_hidden.astype(f32), axis=0)
        grad_up = as_blocks(dot(lifted_all, grad_hidden, 0, 0).astype(bf16))
        streams = [
            Stream([grad_down], "xy" if layer else "XY"),
            Stream([grad_up], "yx" if layer else "YX"),
        ]
        if later:
            grad_hidden = settle(grad_hidden, *later[:2])
            send(*later[:2])
        send(*streams)
        grad_lifted = core_scatter(dot(grad_hidden, w_up, 1, 1))
        grad_low_two, grad_gain_two, grad_shift_two = norm_backward(
            grad_lifted, scaled_two, inverse_two, full_gains[layer, 1]
        )
        grad_middle = grad_stream + grad_low_two
        grad_out_shift = jnp.sum(grad_middle, axis=0)
        attn_grad = core_gather(grad_middle.astype(bf16))
        grad_out = dot(attn_grad, mixture, 0, 0).astype(bf16)
        grad_mixture = dot(attn_grad, w_out, 1, 0).astype(bf16)
        if later:
            grad_mixture = settle(grad_mixture, *later[:2])
            send(*later[:2])
        grad_queries, grad_keys, grad_values = attend_back(
            queries, pair, log_sum, mixture, grad_mixture
        )
        grad_pair = jnp.concatenate([grad_keys, grad_values], axis=1)
        if later:
            grad_pair = settle(grad_pair, *streams, later[2])
            send(*streams, later[2])
        away = core_scatter(dot(grad_pair[own:], w_kv, 1, 1)).astype(bf16)
        if layer > 0:
            away = settle(away, *streams)
            send(*streams)
        away = swap_zl(away)
        grad_in_q = dot(normed_all[:own], grad_queries, 0, 0).astype(bf16)
        grad_in_kv = dot(normed_all, grad_pair, 0, 0).astype(bf16)
        grad_normed = core_scatter(dot(grad_queries, w_q, 1, 1) + dot(grad_pair[:own], w_kv, 1, 1))
        if layer > 0:
            grad_in_q = tie(grad_in_q, away)
        parts = [grad_in_q, grad_in_kv[:, :384], grad_in_kv[:, 384:], grad_out]
        part_q, part_k, part_v, part_o = [as_blocks(part) for part in parts]
        if layer > 0:
            attn = [Stream([part_q, part_k, part_v, part_o], "zXY")]
            later = streams + attn
        else:
            attn = [Stream([part_q, part_o], "XY"), Stream([part_k, part_v], "YX")]
            send(*attn)
            grad_normed = settle(grad_normed, *attn, later[2])
            send(*attn, later[2])
        grad_normed = grad_normed + away.astype(f32)
        grad_low_one, grad_gain_one, grad_shift_one = norm_backward(
            grad_normed, scaled_one, inverse_one, full_gains[layer, 0]
        )
        grad_stream = grad_middle + grad_low_one

        bias_sums = jnp.stack(
            [
                jnp.sum(grad_queries.astype(f32), axis=0),
                jnp.sum(grad_pair[:, 384:].astype(f32), axis=0),
            ]
        )
        vectors.append(
            [
                grad_gain_one,
                grad_gain_two,
                grad_shift_one,
                grad_out_shift,
                grad_shift_two,
                grad_down_shift,
            ]
        )
        up_sums.append(grad_up_bias)
        in_sums.append(bias_sums)
    in_sums = settle(jnp.concatenate(in_sums), *streams, *attn, *later)
    streams = [join(streams[0], attn[0], later[2]), join(streams[1], attn[1])]
    for part in streams:
        in_sums, vectors, up_sums = part.send((in_sums, vectors, up_sums))
    spread = lax.dot_general(
        jnp.concatenate([in_sums[:, :192], in_sums[:, 192:]]),
        narrow_rows(),
        (((1,), (1,)), ((), ())),
        precision=lax.Precision.HIGHEST,
        preferred_element_type=f32,
    )
    small = [jnp.pad(sums[None], ((0, 7), (0, 0))) for sums in vectors[0] + vectors[1]]
    small.append(spread)
    small += [jnp.pad(sums.reshape(2, D), ((0, 6), (0, 0))) for sums in up_sums]
    small.append(jnp.zeros((8, D), f32))
    small = settle(jnp.concatenate(small).T.reshape(16, D // 16, 128), *streams)
    for part in streams:
        small = part.send(small)
    small = jnp.sum(lax.all_to_all(small, ("x", "y"), 0, 0, tiled=True), axis=0)
    small = sum_direct(settle(small, *streams))
    pieces = last_step([*streams, *later[:2]])
    down_0, q_0, o_0, up_0, k_0, v_0, down_1, up_1, q_1, k_1, v_1, o_1 = pieces
    side = lax.axis_index("zl")
    shared = lax.psum(small[:, :96].reshape(rows, 12, 8)[:, :, 0], "core")
    shared = lax.dynamic_slice_in_dim(shared, own_place, 6, 0).T.reshape(2, 6, 6)[::-1]
    grad_gains = shared[:, :2]
    grad_shifts = shared[:, 2:]
    grad_in_bias = lax.dynamic_slice(small, (0, 96 + 4 * side), (6, 4)).T.reshape(2, 2, 6)[::-1]
    grad_up_bias = [lax.dynamic_slice_in_dim(small, at + side, 1, 1) for at in (112, 104)]
    grad_up_bias = jnp.concatenate(grad_up_bias, axis=1).T

    grad_down = jnp.stack([down_0.T, down_1.T])
    grad_up = jnp.stack([up_0, up_1])
    grad_in = jnp.stack([q_0, k_0, v_0, q_1, k_1, v_1])
    grad_in = grad_in.reshape(layers, 3, rows, 192)
    grad_out = jnp.stack([o_0.T, o_1.T])
    return (
        stream,
        grad_stream,
        grad_in,
        grad_in_bias,
        grad_out,
        grad_up,
        grad_up_bias,
        grad_down,
        grad_gains,
        grad_shifts,
    )


def solution(mesh):
    chips = Mesh(mesh.devices.reshape(4, 4, 2, 2, 2), ALL)
    dp, tensor = ("x", "y", "zh"), ("zl", "core")
    both = dp + tensor
    in_specs = (
        P(both, None),
        P(both, None),
        P(None, None, dp, tensor),
        P(None, None, tensor + dp),
        P(None, tensor, dp),
        P(None, dp, tensor),
        P(None, tensor + dp),
        P(None, tensor, dp),
        P(None, None, both),
        P(None, None, both),
    )
    out_specs = (P(both, None), P(both, None)) + in_specs[2:]
    return jax.shard_map(
        per_device, mesh=chips, in_specs=in_specs, out_specs=out_specs, check_vma=False
    )
```
